32 devices in a mesh: grp: 2 (over x), dap: 16 (over z, y, core), ch: 1.
Axes of the slice: x: 2, y: 2, z: 4, core: 2. Of those that a mesh axis runs over, the one named last changes fastest.
Arguments:
- pair: bfloat16 [256, 128, 128], P(('grp', 'dap')), parts along dimension 0, may hold values from -6 to 6
- cotangent: bfloat16 [256, 128, 128], P(('grp', 'dap')), parts along dimension 0, may hold values from -6 to 6
- pair_mask: int32 [256, 128], P(('grp', 'dap')), parts along dimension 0, may hold values 0 or 1
- w_a_gate: bfloat16 [128, 128], P(None, 'ch'), may hold values from -0.5 to 0.5
- w_a_proj: bfloat16 [128, 128], P(None, 'ch'), may hold values from -0.5 to 0.5
- w_b_gate: bfloat16 [128, 128], P(None, 'ch'), may hold values from -0.5 to 0.5
- w_b_proj: bfloat16 [128, 128], P(None, 'ch'), may hold values from -0.5 to 0.5
- w_gate: bfloat16 [128, 128], replicated, may hold values from -0.5 to 0.5
- w_out: bfloat16 [128, 128], P('ch'), may hold values from -0.5 to 0.5
Outputs:
- pair_grad: float32 [256, 128, 128], P(('grp', 'dap')), parts along dimension 0
The draws below stay inside these ranges and needn't reach their ends.
There are 2 independent parts, one for each index of `grp`. The reference program is written for one: setup_inputs(seed, part) draws one part's arguments, and reference() takes and returns one part's arrays. A program takes and returns all parts, laid end to end along the dimension named above; an argument that names none is the same for every part. Nothing has to cross between parts.
All inputs are finite; a program needn't handle non-finite values. No bound on the sum of `pair_mask` on one device may be relied on, other than what follows from the above.
Results may differ from the reference program's by a relative error of at most 0.0068.
Values may be sent and summed in bfloat16 or wider, within the bound.
A program may use at most 128 MiB of HBM per device.

```python
import jax
import jax.numpy as jnp
from jax import lax

C = 128
H = 128
N = 128


def set_ends(drawn, stream_key, smallest, high):
    longest = drawn.shape.index(max(drawn.shape))
    spots = []
    for shift in (0, 1):
        where = [jax.random.randint(jax.random.fold_in(stream_key, axis), (), 0, length) for axis, length in enumerate(drawn.shape)]
        where[longest] = (where[longest] + shift) % drawn.shape[longest]
        spots.append(tuple(where))
    return drawn.at[spots[0]].set(smallest).at[spots[1]].set(high)


def spiked(result, rng, source, target, blocks, factor):
    def block_of(axis_at):
        return (jnp.arange(result.shape[axis_at]) // (result.shape[axis_at] // blocks)).reshape((-1,) + (1,) * (result.ndim - 1 - axis_at))

    near = jax.random.permutation(rng, blocks)[block_of(target)]
    far = (block_of(target) + blocks // 2) % blocks
    return jnp.where((block_of(source) == near) | (block_of(source) == far), factor * result, result)


def block_scale(stream_key, dims, pieces, least, top_value):
    loudness, own = 1.0, jax.random.fold_in(stream_key, 6)
    for position, parts in pieces:
        steps = jnp.exp(jax.random.uniform(jax.random.fold_in(own, position), (parts,), jnp.float32, least / len(pieces), top_value / len(pieces)))
        loudness = loudness * jnp.repeat(steps, dims[position] // parts).reshape([-1 if axis == position else 1 for axis in range(len(dims))])
    return loudness


def scatter_about(own_key, extent, deviation, limit, pieces=(), held_as=jnp.bfloat16):
    drawn = jax.random.normal(own_key, extent, jnp.float32) * deviation
    if len(pieces) > 0:
        drawn = block_scale(own_key, extent, pieces, -0.22, 0.18) * drawn
    return jnp.clip(drawn, min=-limit, max=limit).astype(held_as)


def heavy_noise(own_key, dims, width, reach, pieces, heavy, held_as=jnp.bfloat16):
    drawn = width * jax.random.normal(own_key, dims, jnp.float32)
    if pieces:
        drawn = drawn * block_scale(own_key, dims, pieces, -0.22, 0.18)
    return jnp.clip(spiked(drawn, jax.random.fold_in(own_key, 3), *heavy), -reach, reach).astype(held_as)


def setup_inputs(seed: int = 0, part: int = 0) -> dict:
    splits = jax.random.split(jax.random.key(seed), 10)
    own_keys = jax.random.split(jax.random.fold_in(splits[9], part), 10)
    return {
        "pair": scatter_about(own_keys[0], (N, N, C), 1.0, 6.0, ((0, 16),)),
        "cotangent": heavy_noise(own_keys[1], (N, N, C), 1.0, 6.0, ((0, 16),), (0, 1, 16, 2.0)),
        "pair_mask": set_ends((jax.random.randint(own_keys[2], (N, N), 0, 8) < 7).astype(jnp.int32), jax.random.fold_in(own_keys[2], 1), 0, 1),
        "w_a_gate": scatter_about(splits[3], (C, H), C ** -0.5, 0.5),
        "w_a_proj": scatter_about(splits[4], (C, H), C ** -0.5, 0.5),
        "w_b_gate": scatter_about(splits[5], (C, H), C ** -0.5, 0.5),
        "w_b_proj": scatter_about(splits[6], (C, H), C ** -0.5, 0.5),
        "w_gate": scatter_about(splits[7], (C, C), C ** -0.5, 0.5),
        "w_out": scatter_about(splits[8], (H, C), H ** -0.5, 0.5),
    }


def matmul(left, right):
    return jnp.dot(left, right, preferred_element_type=jnp.float32)

def reference(pair, cotangent, pair_mask, w_a_gate, w_a_proj, w_b_gate, w_b_proj, w_gate, w_out):
    pair_f = pair.astype(jnp.float32)
    mean_c = lax.optimization_barrier(jnp.mean(pair_f, axis=-1, keepdims=True))
    inv_std = jax.lax.rsqrt(lax.optimization_barrier(jnp.mean(pair_f * pair_f, axis=-1, keepdims=True)) - mean_c * mean_c + 1e-05)
    normed = (pair_f - mean_c) * inv_std
    normed_b = normed.astype(jnp.bfloat16)
    masked = pair_mask.astype(jnp.float32)[:, :, None]
    a_gate = jax.nn.sigmoid(matmul(normed_b, w_a_gate))
    a_proj = matmul(normed_b, w_a_proj)
    b_gate = jax.nn.sigmoid(matmul(normed_b, w_b_gate))
    b_proj = matmul(normed_b, w_b_proj)
    left = (a_gate * a_proj * masked).astype(jnp.bfloat16)
    right = (b_gate * b_proj * masked).astype(jnp.bfloat16)
    tri = jnp.einsum('ikc,jkc->ijc', left.astype(jnp.float32), right.astype(jnp.float32))
    mean_h = lax.optimization_barrier(jnp.mean(tri, axis=-1, keepdims=True))
    inv_h = jax.lax.rsqrt(lax.optimization_barrier(jnp.mean(tri * tri, axis=-1, keepdims=True)) - mean_h * mean_h + 1e-05)
    tri_n = (tri - mean_h) * inv_h
    update = matmul(tri_n.astype(jnp.bfloat16), w_out)
    gate = jax.nn.sigmoid(matmul(normed_b, w_gate))
    cot_f = cotangent.astype(jnp.float32)
    d_upd = cot_f * gate
    d_gate_pre = cot_f * update * gate * (1.0 - gate)
    d_trin = matmul(d_upd.astype(jnp.bfloat16), w_out.T)
    d_tri = inv_h * (d_trin - lax.optimization_barrier(jnp.mean(d_trin, axis=-1, keepdims=True)) - tri_n * lax.optimization_barrier(jnp.mean(d_trin * tri_n, axis=-1, keepdims=True)))
    d_tri = d_tri.astype(jnp.bfloat16).astype(jnp.float32)
    d_left = jnp.einsum('ijc,jkc->ikc', d_tri, right.astype(jnp.float32))
    d_right = jnp.einsum('ijc,ikc->jkc', d_tri, left.astype(jnp.float32))
    dla = (d_left * a_proj * masked * a_gate * (1.0 - a_gate)).astype(jnp.bfloat16)
    dlp = (d_left * a_gate * masked).astype(jnp.bfloat16)
    drb = (d_right * b_proj * masked * b_gate * (1.0 - b_gate)).astype(jnp.bfloat16)
    drp = (d_right * b_gate * masked).astype(jnp.bfloat16)
    d_normed = matmul(dla, w_a_gate.T) + matmul(dlp, w_a_proj.T) + matmul(drb, w_b_gate.T) + matmul(drp, w_b_proj.T) + matmul(d_gate_pre.astype(jnp.bfloat16), w_gate.T)
    return inv_std * (d_normed - lax.optimization_barrier(jnp.mean(d_normed, axis=-1, keepdims=True)) - normed * lax.optimization_barrier(jnp.mean(d_normed * normed, axis=-1, keepdims=True)))
```

```python
import functools

import jax
import jax.numpy as jnp
from jax import lax
from jax.experimental import pallas as pl
from jax.experimental.pallas import tpu as pltpu
from jax.sharding import PartitionSpec as P

F32, BF16 = jnp.float32, jnp.bfloat16
ROWS = 8


def matmul(left, right):
    return jnp.dot(left, right, preferred_element_type=jnp.float32)


def shards(pair, cotangent, pair_mask, w_a_gate, w_a_proj, w_b_gate, w_b_proj, w_gate, w_out):
    hidden_all = w_out.shape[0] * lax.axis_size("ch")
    pair_f = pair.astype(jnp.float32)
    mean_c = jnp.mean(pair_f, axis=-1, keepdims=True)
    inv_std = lax.rsqrt(jnp.mean(pair_f * pair_f, axis=-1, keepdims=True) - mean_c * mean_c + 1e-05)
    normed = (pair_f - mean_c) * inv_std
    normed_b = normed.astype(jnp.bfloat16)
    masked = pair_mask.astype(jnp.float32)[:, :, None]
    a_gate = jax.nn.sigmoid(matmul(normed_b, w_a_gate))
    a_proj = matmul(normed_b, w_a_proj)
    b_gate = jax.nn.sigmoid(matmul(normed_b, w_b_gate))
    b_proj = matmul(normed_b, w_b_proj)
    left = (a_gate * a_proj * masked).astype(jnp.bfloat16)
    right = (b_gate * b_proj * masked).astype(jnp.bfloat16)
    right_all = lax.all_gather(right, "dap", axis=0, tiled=True)
    tri = jnp.einsum("ikc,jkc->ijc", left, right_all, preferred_element_type=jnp.float32)
    sum_one, sum_two = lax.psum((jnp.sum(tri, axis=-1), jnp.sum(tri * tri, axis=-1)), "ch")
    mean_h = (sum_one / hidden_all)[:, :, None]
    inv_h = lax.rsqrt((sum_two / hidden_all)[:, :, None] - mean_h * mean_h + 1e-05)
    tri_n = (tri - mean_h) * inv_h
    update = lax.psum(matmul(tri_n.astype(jnp.bfloat16), w_out).astype(jnp.bfloat16), "ch").astype(
        jnp.float32
    )
    gate = jax.nn.sigmoid(matmul(normed_b, w_gate))
    cot_f = cotangent.astype(jnp.float32)
    d_upd = cot_f * gate
    d_gate_pre = cot_f * update * gate * (1.0 - gate)
    d_trin = matmul(d_upd.astype(jnp.bfloat16), w_out.T)
    grad_one, grad_two = lax.psum(
        (jnp.sum(d_trin, axis=-1), jnp.sum(d_trin * tri_n, axis=-1)), "ch"
    )
    d_tri = inv_h * (
        d_trin - (grad_one / hidden_all)[:, :, None] - tri_n * (grad_two / hidden_all)[:, :, None]
    )
    d_tri = d_tri.astype(jnp.bfloat16)
    d_left = jnp.einsum("ijc,jkc->ikc", d_tri, right_all, preferred_element_type=jnp.float32)
    d_right = lax.psum_scatter(
        jnp.einsum("ijc,ikc->jkc", d_tri, left, preferred_element_type=jnp.float32),
        "dap",
        scatter_dimension=0,
        tiled=True,
    )
    dla = (d_left * a_proj * masked * a_gate * (1.0 - a_gate)).astype(jnp.bfloat16)
    dlp = (d_left * a_gate * masked).astype(jnp.bfloat16)
    drb = (d_right * b_proj * masked * b_gate * (1.0 - b_gate)).astype(jnp.bfloat16)
    drp = (d_right * b_gate * masked).astype(jnp.bfloat16)
    partial_grad = (
        matmul(dla, w_a_gate.T)
        + matmul(dlp, w_a_proj.T)
        + matmul(drb, w_b_gate.T)
        + matmul(drp, w_b_proj.T)
    )
    d_normed = lax.psum(partial_grad, "ch") + matmul(d_gate_pre.astype(jnp.bfloat16), w_gate.T)
    return inv_std * (
        d_normed
        - jnp.mean(d_normed, axis=-1, keepdims=True)
        - normed * jnp.mean(d_normed * normed, axis=-1, keepdims=True)
    )


def transposed(w):
    return w[...].astype(F32).T


def interleaved(w_a, w_b, n):
    width = w_a.shape[0]
    both = jnp.concatenate(
        [transposed(w_a).reshape(n, ROWS, width), transposed(w_b).reshape(n, ROWS, width)], axis=1
    )
    return both.reshape(2 * n * ROWS, width)


def fused_kernel(
    n, pair, cotangent, pair_mask, w_a_gate, w_a_proj, w_b_gate, w_b_proj, w_gate, w_out, out,
    normed_s, inv_s, gate_s, proj_s, og_s, dtrin_s, dpre_s, pos_buf, both_s, tri_s, grad_s,
    send1, recv1, send2, recv2, send3, recv3, send4, recv4, send_sem, recv_sem,
):
    me = lax.axis_index("dap")
    chans = w_out.shape[0]
    length = pair.shape[1]

    def peer_of(off):
        return lax.rem(me + off, n)

    def source_of(off):
        return lax.rem(me + n - off, n)

    def copy_to(phase, send, recv, off):
        peer = peer_of(off)
        return pltpu.make_async_remote_copy(
            src_ref=send.at[peer],
            dst_ref=recv.at[me],
            send_sem=send_sem.at[phase, off],
            recv_sem=recv_sem.at[phase, off],
            device_id={"dap": peer},
            device_id_type=pl.DeviceIdType.MESH,
        )

    def exchange(phase, send, recv, block, unpack, meanwhile=None):
        @pl.loop(1, n)
        def _(off):
            peer = peer_of(off)
            send[peer] = block(peer).astype(BF16)
            copy_to(phase, send, recv, off).start()

        unpack(me, block(me).astype(BF16).astype(F32))
        if meanwhile is not None:
            meanwhile()

        @pl.loop(1, n)
        def _(off):
            copy_to(phase, send, recv, off).wait_recv()
            source = source_of(off)
            unpack(source, recv[source].astype(F32))

    barrier = pltpu.get_barrier_semaphore()

    @pl.loop(1, n)
    def _(off):
        pl.semaphore_signal(
            barrier, inc=1, device_id={"dap": peer_of(off)}, device_id_type=pl.DeviceIdType.MESH
        )

    gate_t = interleaved(w_a_gate, w_b_gate, n)
    proj_t = interleaved(w_a_proj, w_b_proj, n)
    gate_tb, proj_tb = gate_t.astype(BF16), proj_t.astype(BF16)
    for i in range(ROWS):
        x = pair[i].astype(F32).T
        mu = jnp.mean(x, axis=0, keepdims=True)
        inv = lax.rsqrt(jnp.mean(x * x, axis=0, keepdims=True) - mu * mu + 1e-05)
        normed = (x - mu) * inv
        normed_s[i] = normed
        inv_s[i] = inv
        normed_b = normed.astype(BF16)
        gate = jax.nn.sigmoid(matmul(gate_tb, normed_b))
        proj = matmul(proj_tb, normed_b)
        gate_s[i] = gate
        proj_s[i] = proj
        masked = pair_mask[i : i + 1, :].astype(F32)
        pos_buf[pl.ds(i, 2 * chans, stride=ROWS), :] = gate * proj * masked
    pl.semaphore_wait(barrier, n - 1)

    def rows_of(count):
        size = count * ROWS
        return lambda d: pos_buf[pl.ds(pl.multiple_of(d * size, size), size), :]

    def to_channels(buf, count):
        def unpack(s, values):
            buf[:, pl.ds(pl.multiple_of(s * ROWS, ROWS), ROWS), :] = values.reshape(
                count, ROWS, length
            )

        return unpack

    def from_channels(buf, count):
        return lambda d: buf[:, pl.ds(pl.multiple_of(d * ROWS, ROWS), ROWS), :].reshape(
            count * ROWS, length
        )

    def to_rows(count):
        size = count * ROWS

        def unpack(s, values):
            pos_buf[pl.ds(pl.multiple_of(s * size, size), size), :] = values

        return unpack

    def output_side():
        og_t = transposed(w_gate).astype(BF16)
        for i in range(ROWS):
            gate = jax.nn.sigmoid(matmul(og_t, normed_s[i].astype(BF16)))
            d_upd = cotangent[i].astype(F32).T * gate
            dtrin_s[i] = matmul(w_out[...], d_upd.astype(BF16))
            og_s[i] = d_upd * (1.0 - gate)

    exchange(0, send1, recv1, rows_of(2 * ROWS), to_channels(both_s, 2 * ROWS), output_side)

    for c in range(ROWS):
        tri_s[c] = lax.dot_general(
            both_s[c].astype(BF16),
            both_s[ROWS + c].astype(BF16),
            (((1,), (1,)), ((), ())),
            preferred_element_type=F32,
        )
    exchange(1, send2, recv2, from_channels(tri_s, ROWS), to_rows(ROWS))

    out_t = transposed(w_out).astype(BF16)
    for i in range(ROWS):
        rows = pl.ds(i, chans, stride=ROWS)
        tri = pos_buf[rows, :]
        mean_h = jnp.mean(tri, axis=0, keepdims=True)
        inv_h = lax.rsqrt(jnp.mean(tri * tri, axis=0, keepdims=True) - mean_h * mean_h + 1e-05)
        tri_n = (tri - mean_h) * inv_h
        update = matmul(out_t, tri_n.astype(BF16))
        dpre_s[i] = (og_s[i] * update).astype(BF16)
        d_trin = dtrin_s[i]
        one = jnp.mean(d_trin, axis=0, keepdims=True)
        two = jnp.mean(d_trin * tri_n, axis=0, keepdims=True)
        pos_buf[rows, :] = inv_h * (d_trin - one - tri_n * two)

    exchange(2, send3, recv3, rows_of(ROWS), to_channels(tri_s, ROWS))

    for c in range(ROWS):
        d_tri = tri_s[c]
        grad_s[c] = matmul(d_tri.astype(BF16), both_s[ROWS + c].astype(BF16))
        grad_s[ROWS + c] = matmul(d_tri.T.astype(BF16), both_s[c].astype(BF16))

    exchange(3, send4, recv4, from_channels(grad_s, 2 * ROWS), to_rows(2 * ROWS))

    gate_w, proj_w = gate_t.T.astype(BF16), proj_t.T.astype(BF16)
    for i in range(ROWS):
        grad = pos_buf[pl.ds(i, 2 * chans, stride=ROWS), :] * pair_mask[i : i + 1, :].astype(F32)
        gate = gate_s[i]
        d_proj = grad * gate
        d_gate = d_proj * proj_s[i] * (1.0 - gate)
        d_normed = (
            matmul(gate_w, d_gate.astype(BF16))
            + matmul(proj_w, d_proj.astype(BF16))
            + matmul(w_gate[...], dpre_s[i])
        )
        normed = normed_s[i]
        out[i] = inv_s[i] * (
            d_normed
            - jnp.mean(d_normed, axis=0, keepdims=True)
            - normed * jnp.mean(d_normed * normed, axis=0, keepdims=True)
        )

    for phase, send, recv in ((0, send1, recv1), (1, send2, recv2), (2, send3, recv3), (3, send4, recv4)):

        @pl.loop(1, n)
        def _(off):
            copy_to(phase, send, recv, off).wait_send()


def fused_shards(n, pair, *rest):
    rows, length, chans = pair.shape
    wide, narrow = 2 * ROWS * ROWS, ROWS * ROWS
    grad_t = pl.pallas_call(
        functools.partial(fused_kernel, n),
        out_shape=jax.ShapeDtypeStruct((rows, chans, length), F32),
        in_specs=[pl.BlockSpec(memory_space=pltpu.VMEM)] * 9,
        out_specs=pl.BlockSpec(memory_space=pltpu.VMEM),
        scratch_shapes=[
            pltpu.VMEM((rows, chans, length), F32),
            pltpu.VMEM((rows, 1, length), F32),
            pltpu.VMEM((rows, 2 * chans, length), F32),
            pltpu.VMEM((rows, 2 * chans, length), F32),
            pltpu.VMEM((rows, chans, length), F32),
            pltpu.VMEM((rows, chans, length), F32),
            pltpu.VMEM((rows, chans, length), BF16),
            pltpu.VMEM((2 * chans * rows, length), F32),
            pltpu.VMEM((2 * ROWS, length, length), F32),
            pltpu.VMEM((ROWS, length, length), F32),
            pltpu.VMEM((2 * ROWS, length, length), F32),
            pltpu.VMEM((n, wide, length), BF16),
            pltpu.VMEM((n, wide, length), BF16),
            pltpu.VMEM((n, narrow, length), BF16),
            pltpu.VMEM((n, narrow, length), BF16),
            pltpu.VMEM((n, narrow, length), BF16),
            pltpu.VMEM((n, narrow, length), BF16),
            pltpu.VMEM((n, wide, length), BF16),
            pltpu.VMEM((n, wide, length), BF16),
            pltpu.SemaphoreType.DMA((4, n)),
            pltpu.SemaphoreType.DMA((4, n)),
        ],
        compiler_params=pltpu.CompilerParams(
            collective_id=0, has_side_effects=True, vmem_limit_bytes=48 * 1024 * 1024
        ),
    )(pair, *rest)
    return jnp.swapaxes(grad_t, 1, 2)


def body_for(mesh):
    n = mesh.shape["dap"]

    def body(pair, *rest):
        rows, length, chans = pair.shape
        fits = mesh.shape["ch"] == 1 and n > 1 and rows == ROWS and chans == n * ROWS
        if fits and length == rows * n == 128:
            return fused_shards(n, pair, *rest)
        return shards(pair, *rest)

    return body


def solution(mesh):
    return jax.shard_map(
        body_for(mesh),
        mesh=mesh,
        in_specs=(
            P(("grp", "dap"), None, None),
            P(("grp", "dap"), None, None),
            P(("grp", "dap"), None),
            P(None, "ch"),
            P(None, "ch"),
            P(None, "ch"),
            P(None, "ch"),
            P(),
            P("ch", None),
        ),
        out_specs=P(("grp", "dap"), None, None),
        check_vma=False,
    )
```

```python
import functools

import jax
import jax.numpy as jnp
from jax import lax
from jax.experimental import pallas as pl
from jax.experimental.pallas import tpu as pltpu
from jax.sharding import PartitionSpec as P

F32, BF16 = jnp.float32, jnp.bfloat16
ROWS = 8


def matmul(left, right):
    return jnp.dot(left, right, preferred_element_type=jnp.float32)


def shards(pair, cotangent, pair_mask, w_a_gate, w_a_proj, w_b_gate, w_b_proj, w_gate, w_out):
    hidden_all = w_out.shape[0] * lax.axis_size("ch")
    pair_f = pair.astype(jnp.float32)
    mean_c = jnp.mean(pair_f, axis=-1, keepdims=True)
    inv_std = lax.rsqrt(jnp.mean(pair_f * pair_f, axis=-1, keepdims=True) - mean_c * mean_c + 1e-05)
    normed = (pair_f - mean_c) * inv_std
    normed_b = normed.astype(jnp.bfloat16)
    masked = pair_mask.astype(jnp.float32)[:, :, None]
    a_gate = jax.nn.sigmoid(matmul(normed_b, w_a_gate))
    a_proj = matmul(normed_b, w_a_proj)
    b_gate = jax.nn.sigmoid(matmul(normed_b, w_b_gate))
    b_proj = matmul(normed_b, w_b_proj)
    left = (a_gate * a_proj * masked).astype(jnp.bfloat16)
    right = (b_gate * b_proj * masked).astype(jnp.bfloat16)
    right_all = lax.all_gather(right, "dap", axis=0, tiled=True)
    tri = jnp.einsum("ikc,jkc->ijc", left, right_all, preferred_element_type=jnp.float32)
    sum_one, sum_two = lax.psum((jnp.sum(tri, axis=-1), jnp.sum(tri * tri, axis=-1)), "ch")
    mean_h = (sum_one / hidden_all)[:, :, None]
    inv_h = lax.rsqrt((sum_two / hidden_all)[:, :, None] - mean_h * mean_h + 1e-05)
    tri_n = (tri - mean_h) * inv_h
    update = lax.psum(matmul(tri_n.astype(jnp.bfloat16), w_out).astype(jnp.bfloat16), "ch").astype(
        jnp.float32
    )
    gate = jax.nn.sigmoid(matmul(normed_b, w_gate))
    cot_f = cotangent.astype(jnp.float32)
    d_upd = cot_f * gate
    d_gate_pre = cot_f * update * gate * (1.0 - gate)
    d_trin = matmul(d_upd.astype(jnp.bfloat16), w_out.T)
    grad_one, grad_two = lax.psum(
        (jnp.sum(d_trin, axis=-1), jnp.sum(d_trin * tri_n, axis=-1)), "ch"
    )
    d_tri = inv_h * (
        d_trin - (grad_one / hidden_all)[:, :, None] - tri_n * (grad_two / hidden_all)[:, :, None]
    )
    d_tri = d_tri.astype(jnp.bfloat16)
    d_left = jnp.einsum("ijc,jkc->ikc", d_tri, right_all, preferred_element_type=jnp.float32)
    d_right = lax.psum_scatter(
        jnp.einsum("ijc,ikc->jkc", d_tri, left, preferred_element_type=jnp.float32),
        "dap",
        scatter_dimension=0,
        tiled=True,
    )
    dla = (d_left * a_proj * masked * a_gate * (1.0 - a_gate)).astype(jnp.bfloat16)
    dlp = (d_left * a_gate * masked).astype(jnp.bfloat16)
    drb = (d_right * b_proj * masked * b_gate * (1.0 - b_gate)).astype(jnp.bfloat16)
    drp = (d_right * b_gate * masked).astype(jnp.bfloat16)
    partial_grad = (
        matmul(dla, w_a_gate.T)
        + matmul(dlp, w_a_proj.T)
        + matmul(drb, w_b_gate.T)
        + matmul(drp, w_b_proj.T)
    )
    d_normed = lax.psum(partial_grad, "ch") + matmul(d_gate_pre.astype(jnp.bfloat16), w_gate.T)
    return inv_std * (
        d_normed
        - jnp.mean(d_normed, axis=-1, keepdims=True)
        - normed * jnp.mean(d_normed * normed, axis=-1, keepdims=True)
    )


def transposed(w):
    return w[...].astype(F32).T


def interleaved(w_a, w_b, parts):
    chans, width = w_a.shape[1], w_a.shape[0]
    shape = (parts, chans // parts, width)
    both = jnp.concatenate([transposed(w_a).reshape(shape), transposed(w_b).reshape(shape)], axis=1)
    return both.reshape(2 * chans, width)


def fused_kernel(n, *refs):
    inputs, out, held, refs = refs[:9], refs[9], refs[10:19], refs[19:]
    (
        normed_s, nb_s, inv_s, gate_s, proj_s, og_s, dtrin_s, dpre_s, pos_buf, left_s, right_s, tri_s,
        dleft_s, dright_s, send1, recv1, far1, send2, recv2, send3, recv3, send4, recv4, sfar4, far4,
        send_sem, recv_sem, in_sem,
    ) = refs
    pair, cotangent, pair_mask, w_a_gate, w_a_proj, w_b_gate, w_b_proj, w_gate, w_out = held
    chans = w_out.shape[0]
    length = pair.shape[1]
    parts = n // 2
    width = chans // parts
    block = width * ROWS
    me = lax.axis_index("dap")
    mine = lax.rem(me, parts)
    own_base = me - mine
    far_base = parts - own_base

    loads = [pltpu.make_async_copy(inputs[x], held[x], in_sem.at[x]) for x in range(9)]
    for load in loads:
        load.start()

    barrier = pltpu.get_barrier_semaphore()

    @pl.loop(1, n)
    def _(off):
        pl.semaphore_signal(
            barrier,
            inc=1,
            device_id={"dap": lax.rem(me + off, n)},
            device_id_type=pl.DeviceIdType.MESH,
        )

    def copy(phase, far, src, dst, to, source):
        base, slot = (far_base, parts) if far else (own_base, 0)
        return pltpu.make_async_remote_copy(
            src_ref=src,
            dst_ref=dst,
            send_sem=send_sem.at[phase, slot + to],
            recv_sem=recv_sem.at[phase, slot + source],
            device_id={"dap": base + to},
            device_id_type=pl.DeviceIdType.MESH,
        )

    def turn(t):
        return lax.rem(mine + t, parts)

    def at_rows(d):
        return pl.ds(pl.multiple_of(d * ROWS, ROWS), ROWS)

    def at_blocks(d, size):
        return pl.ds(pl.multiple_of(d * size, size), size)

    def grouped(values):
        return values.reshape(values.shape[0] // ROWS, ROWS, length)

    for load in loads:
        load.wait()
    gate_t = interleaved(w_a_gate, w_b_gate, parts)
    proj_t = interleaved(w_a_proj, w_b_proj, parts)
    gate_tb, proj_tb = gate_t.astype(BF16), proj_t.astype(BF16)
    for i in range(ROWS):
        x = pair[i].astype(F32).T
        mu = jnp.mean(x, axis=0, keepdims=True)
        inv = lax.rsqrt(jnp.mean(x * x, axis=0, keepdims=True) - mu * mu + 1e-05)
        normed = (x - mu) * inv
        normed_s[i] = normed
        inv_s[i] = inv
        nb_s[i] = normed.astype(BF16)

    few = parts // 2
    for g in range(2):
        rows = slice(g * chans, (g + 1) * chans)
        for i in range(ROWS):
            gate = jax.nn.sigmoid(matmul(gate_tb[rows], nb_s[i]))
            proj = matmul(proj_tb[rows], nb_s[i])
            gate_s[i, rows] = gate
            proj_s[i, rows] = proj
            masked = pair_mask[i : i + 1, :].astype(F32)
            pos_buf[pl.ds(g * chans * ROWS + i, chans, stride=ROWS), :] = gate * proj * masked
        if g == 0:
            pl.semaphore_wait(barrier, n - 1)

        @pl.loop(0, few)
        def _(t):
            q = g * few + lax.rem(mine + t, few)
            send1[q] = pos_buf[at_blocks(q, 2 * block), :].astype(BF16)
            copy(0, True, send1.at[q, pl.ds(block, block)], far1.at[mine], q, mine).start()

            @pl.when(q != mine)
            def _():
                copy(0, False, send1.at[q], recv1.at[mine], q, mine).start()

    og_t = transposed(w_gate).astype(BF16)
    for i in range(ROWS):
        gate = jax.nn.sigmoid(matmul(og_t, nb_s[i]))
        d_upd = cotangent[i].astype(F32).T * gate
        dtrin_s[i] = matmul(w_out[...], d_upd.astype(BF16))
        og_s[i] = d_upd * (1.0 - gate)

    def keep(s, values):
        values = grouped(values.astype(F32))
        left_s[:, at_rows(s), :] = values[:width]
        right_s[:, at_rows(own_base + s), :] = values[width:]

    keep(mine, send1[mine])

    @pl.loop(1, parts)
    def _(t):
        s = turn(t)
        copy(0, False, send1.at[s], recv1.at[s], s, s).wait_recv()
        keep(s, recv1[s])

    @pl.loop(0, parts)
    def _(t):
        s = turn(t)
        copy(0, True, send1.at[s, pl.ds(block, block)], far1.at[s], s, s).wait_recv()
        right_s[:, at_rows(far_base + s), :] = grouped(far1[s].astype(F32))

    for c in range(width):
        tri_s[c] = lax.dot_general(
            left_s[c].astype(BF16),
            right_s[c].astype(BF16),
            (((1,), (1,)), ((), ())),
            preferred_element_type=F32,
        )

    def tri_block(q):
        return tri_s[:, at_rows(q), :].reshape(block, length)

    @pl.loop(1, parts)
    def _(t):
        q = turn(t)
        send2[q] = tri_block(q).astype(BF16)
        copy(1, False, send2.at[q], recv2.at[mine], q, mine).start()

    pos_buf[at_blocks(mine, block), :] = tri_block(mine)

    @pl.loop(1, parts)
    def _(t):
        s = turn(t)
        copy(1, False, send2.at[s], recv2.at[s], s, s).wait_recv()
        pos_buf[at_blocks(s, block), :] = recv2[s].astype(F32)

    out_t = transposed(w_out).astype(BF16)
    for i in range(ROWS):
        rows = pl.ds(i, chans, stride=ROWS)
        tri = pos_buf[rows, :]
        mean_h = jnp.mean(tri, axis=0, keepdims=True)
        inv_h = lax.rsqrt(jnp.mean(tri * tri, axis=0, keepdims=True) - mean_h * mean_h + 1e-05)
        tri_n = (tri - mean_h) * inv_h
        update = matmul(out_t, tri_n.astype(BF16))
        dpre_s[i] = (og_s[i] * update).astype(BF16)
        d_trin = dtrin_s[i]
        one = jnp.mean(d_trin, axis=0, keepdims=True)
        two = jnp.mean(d_trin * tri_n, axis=0, keepdims=True)
        pos_buf[rows, :] = inv_h * (d_trin - one - tri_n * two)

    @pl.loop(1, parts)
    def _(t):
        q = turn(t)
        send3[q] = pos_buf[at_blocks(q, block), :].astype(BF16)
        copy(2, False, send3.at[q], recv3.at[mine], q, mine).start()

    tri_s[:, at_rows(mine), :] = grouped(pos_buf[at_blocks(mine, block), :])

    @pl.loop(1, parts)
    def _(t):
        s = turn(t)
        copy(2, False, send3.at[s], recv3.at[s], s, s).wait_recv()
        tri_s[:, at_rows(s), :] = grouped(recv3[s].astype(F32))

    for c in range(width):
        dright_s[c] = matmul(tri_s[c].T.astype(BF16), left_s[c].astype(BF16))

    @pl.loop(0, parts)
    def _(t):
        q = turn(t)
        sfar4[q] = dright_s[:, at_rows(far_base + q), :].reshape(block, length).astype(BF16)
        copy(3, True, sfar4.at[q], far4.at[mine], q, mine).start()

    for c in range(width):
        dleft_s[c] = matmul(tri_s[c].astype(BF16), right_s[c].astype(BF16))

    def grad_blocks(q):
        return (
            dleft_s[:, at_rows(q), :].reshape(block, length),
            dright_s[:, at_rows(own_base + q), :].reshape(block, length),
        )

    @pl.loop(1, parts)
    def _(t):
        q = turn(t)
        d_left, d_right = grad_blocks(q)
        send4[q, pl.ds(0, block)] = d_left.astype(BF16)
        send4[q, pl.ds(block, block)] = d_right.astype(BF16)
        copy(3, False, send4.at[q], recv4.at[mine], q, mine).start()

    d_left, d_right = grad_blocks(mine)
    pos_buf[at_blocks(2 * mine, block), :] = d_left
    pos_buf[at_blocks(2 * mine + 1, block), :] = d_right
    gate_w, proj_w = gate_t.T.astype(BF16), proj_t.T.astype(BF16)

    @pl.loop(1, parts)
    def _(t):
        s = turn(t)
        copy(3, False, send4.at[s], recv4.at[s], s, s).wait_recv()
        pos_buf[at_blocks(s, 2 * block), :] = recv4[s].astype(F32)

    @pl.loop(0, parts)
    def _(t):
        s = turn(t)
        copy(3, True, sfar4.at[s], far4.at[s], s, s).wait_recv()
        pos_buf[at_blocks(2 * s + 1, block), :] += far4[s].astype(F32)

    for i in range(ROWS):
        grad = pos_buf[pl.ds(i, 2 * chans, stride=ROWS), :] * pair_mask[i : i + 1, :].astype(F32)
        gate = gate_s[i]
        d_proj = grad * gate
        d_gate = d_proj * proj_s[i] * (1.0 - gate)
        d_normed = (
            matmul(gate_w, d_gate.astype(BF16))
            + matmul(proj_w, d_proj.astype(BF16))
            + matmul(w_gate[...], dpre_s[i])
        )
        normed = normed_s[i]
        out[i] = inv_s[i] * (
            d_normed
            - jnp.mean(d_normed, axis=0, keepdims=True)
            - normed * jnp.mean(d_normed * normed, axis=0, keepdims=True)
        )

    @pl.loop(0, parts)
    def _(q):
        copy(0, True, send1.at[q, pl.ds(block, block)], far1.at[q], q, q).wait_send()
        copy(3, True, sfar4.at[q], far4.at[q], q, q).wait_send()

    @pl.loop(1, parts)
    def _(t):
        q = turn(t)
        copy(0, False, send1.at[q], recv1.at[q], q, q).wait_send()
        copy(1, False, send2.at[q], recv2.at[q], q, q).wait_send()
        copy(2, False, send3.at[q], recv3.at[q], q, q).wait_send()
        copy(3, False, send4.at[q], recv4.at[q], q, q).wait_send()


def fused_shards(n, *args):
    rows, length, chans = args[0].shape
    parts = n // 2
    width = chans // parts
    block = width * rows

    def vmem(dtype, *shape):
        return pltpu.VMEM(shape, dtype)

    grad_t = pl.pallas_call(
        functools.partial(fused_kernel, n),
        out_shape=jax.ShapeDtypeStruct((rows, chans, length), F32),
        in_specs=[pl.BlockSpec(memory_space=pltpu.HBM)] * 9,
        out_specs=pl.BlockSpec(memory_space=pltpu.VMEM),
        scratch_shapes=[pltpu.VMEM(x.shape, x.dtype) for x in args]
        + [
            vmem(F32, rows, chans, length),
            vmem(BF16, rows, chans, length),
            vmem(F32, rows, 1, length),
            vmem(F32, rows, 2 * chans, length),
            vmem(F32, rows, 2 * chans, length),
            vmem(F32, rows, chans, length),
            vmem(F32, rows, chans, length),
            vmem(BF16, rows, chans, length),
            vmem(F32, 2 * chans * rows, length),
            vmem(F32, width, parts * rows, length),
            vmem(F32, width, length, length),
            vmem(F32, width, parts * rows, length),
            vmem(F32, width, parts * rows, length),
            vmem(F32, width, length, length),
            vmem(BF16, parts, 2 * block, length),
            vmem(BF16, parts, 2 * block, length),
            vmem(BF16, parts, block, length),
            vmem(BF16, parts, block, length),
            vmem(BF16, parts, block, length),
            vmem(BF16, parts, block, length),
            vmem(BF16, parts, block, length),
            vmem(BF16, parts, 2 * block, length),
            vmem(BF16, parts, 2 * block, length),
            vmem(BF16, parts, block, length),
            vmem(BF16, parts, block, length),
            pltpu.SemaphoreType.DMA((4, n)),
            pltpu.SemaphoreType.DMA((4, n)),
            pltpu.SemaphoreType.DMA((9,)),
        ],
        compiler_params=pltpu.CompilerParams(
            collective_id=0, has_side_effects=True, vmem_limit_bytes=48 * 1024 * 1024
        ),
    )(*args)
    return jnp.swapaxes(grad_t, 1, 2)


def body_for(mesh):
    n = mesh.shape["dap"]

    def body(*args):
        rows, length, chans = args[0].shape
        fits = mesh.shape["ch"] == 1 and n == 16 and rows == ROWS
        if fits and length == rows * n == chans:
            return fused_shards(n, *args)
        return shards(*args)

    return body


def solution(mesh):
    return jax.shard_map(
        body_for(mesh),
        mesh=mesh,
        in_specs=(
            P(("grp", "dap"), None, None),
            P(("grp", "dap"), None, None),
            P(("grp", "dap"), None),
            P(None, "ch"),
            P(None, "ch"),
            P(None, "ch"),
            P(None, "ch"),
            P(),
            P("ch", None),
        ),
        out_specs=P(("grp", "dap"), None, None),
        check_vma=False,
    )
```

```python
import functools

import jax
import jax.numpy as jnp
from jax import lax
from jax.experimental import pallas as pl
from jax.experimental.pallas import tpu as pltpu
from jax.sharding import PartitionSpec as P

F32, BF16 = jnp.float32, jnp.bfloat16
ROWS = 8


def matmul(left, right):
    return jnp.dot(left, right, preferred_element_type=jnp.float32)


def shards(pair, cotangent, pair_mask, w_a_gate, w_a_proj, w_b_gate, w_b_proj, w_gate, w_out):
    hidden_all = w_out.shape[0] * lax.axis_size("ch")
    pair_f = pair.astype(jnp.float32)
    mean_c = jnp.mean(pair_f, axis=-1, keepdims=True)
    inv_std = lax.rsqrt(jnp.mean(pair_f * pair_f, axis=-1, keepdims=True) - mean_c * mean_c + 1e-05)
    normed = (pair_f - mean_c) * inv_std
    normed_b = normed.astype(jnp.bfloat16)
    masked = pair_mask.astype(jnp.float32)[:, :, None]
    a_gate = jax.nn.sigmoid(matmul(normed_b, w_a_gate))
    a_proj = matmul(normed_b, w_a_proj)
    b_gate = jax.nn.sigmoid(matmul(normed_b, w_b_gate))
    b_proj = matmul(normed_b, w_b_proj)
    left = (a_gate * a_proj * masked).astype(jnp.bfloat16)
    right = (b_gate * b_proj * masked).astype(jnp.bfloat16)
    right_all = lax.all_gather(right, "dap", axis=0, tiled=True)
    tri = jnp.einsum("ikc,jkc->ijc", left, right_all, preferred_element_type=jnp.float32)
    sum_one, sum_two = lax.psum((jnp.sum(tri, axis=-1), jnp.sum(tri * tri, axis=-1)), "ch")
    mean_h = (sum_one / hidden_all)[:, :, None]
    inv_h = lax.rsqrt((sum_two / hidden_all)[:, :, None] - mean_h * mean_h + 1e-05)
    tri_n = (tri - mean_h) * inv_h
    update = lax.psum(matmul(tri_n.astype(jnp.bfloat16), w_out).astype(jnp.bfloat16), "ch").astype(
        jnp.float32
    )
    gate = jax.nn.sigmoid(matmul(normed_b, w_gate))
    cot_f = cotangent.astype(jnp.float32)
    d_upd = cot_f * gate
    d_gate_pre = cot_f * update * gate * (1.0 - gate)
    d_trin = matmul(d_upd.astype(jnp.bfloat16), w_out.T)
    grad_one, grad_two = lax.psum(
        (jnp.sum(d_trin, axis=-1), jnp.sum(d_trin * tri_n, axis=-1)), "ch"
    )
    d_tri = inv_h * (
        d_trin - (grad_one / hidden_all)[:, :, None] - tri_n * (grad_two / hidden_all)[:, :, None]
    )
    d_tri = d_tri.astype(jnp.bfloat16)
    d_left = jnp.einsum("ijc,jkc->ikc", d_tri, right_all, preferred_element_type=jnp.float32)
    d_right = lax.psum_scatter(
        jnp.einsum("ijc,ikc->jkc", d_tri, left, preferred_element_type=jnp.float32),
        "dap",
        scatter_dimension=0,
        tiled=True,
    )
    dla = (d_left * a_proj * masked * a_gate * (1.0 - a_gate)).astype(jnp.bfloat16)
    dlp = (d_left * a_gate * masked).astype(jnp.bfloat16)
    drb = (d_right * b_proj * masked * b_gate * (1.0 - b_gate)).astype(jnp.bfloat16)
    drp = (d_right * b_gate * masked).astype(jnp.bfloat16)
    partial_grad = (
        matmul(dla, w_a_gate.T)
        + matmul(dlp, w_a_proj.T)
        + matmul(drb, w_b_gate.T)
        + matmul(drp, w_b_proj.T)
    )
    d_normed = lax.psum(partial_grad, "ch") + matmul(d_gate_pre.astype(jnp.bfloat16), w_gate.T)
    return inv_std * (
        d_normed
        - jnp.mean(d_normed, axis=-1, keepdims=True)
        - normed * jnp.mean(d_normed * normed, axis=-1, keepdims=True)
    )


def transposed(w):
    return w[...].astype(F32).T


def interleaved(w_a, w_b, parts):
    chans, width = w_a.shape[1], w_a.shape[0]
    shape = (parts, chans // parts, width)
    both = jnp.concatenate([transposed(w_a).reshape(shape), transposed(w_b).reshape(shape)], axis=1)
    return both.reshape(2 * chans, width)


def fused_kernel(n, *refs):
    packed, out, held, refs = refs[0], refs[1], refs[2], refs[3:]
    (
        normed_s, nb_s, inv_s, gate_s, proj_s, og_s, dtrin_s, dpre_s, pos_buf, left_s, right_s, tri_s,
        dleft_s, dright_s, send1, recv1, far1, send2, recv2, send3, recv3, send4, recv4, sfar4, far4,
        send_sem, recv_sem, in_sem,
    ) = refs
    length = chans = held.shape[1]
    size = ROWS * length
    pair = [held.at[pl.ds(i * length, length)] for i in range(ROWS)]
    cotangent = [held.at[pl.ds(size + i * length, length)] for i in range(ROWS)]
    w_a_gate, w_a_proj, w_b_gate, w_b_proj, w_gate, w_out = [
        held.at[pl.ds(2 * size + x * chans, chans)] for x in range(6)
    ]
    parts = n // 2
    width = chans // parts
    block = width * ROWS
    me = lax.axis_index("dap")
    mine = lax.rem(me, parts)
    own_base = me - mine
    far_base = parts - own_base

    load = pltpu.make_async_copy(packed, held, in_sem)
    load.start()

    barrier = pltpu.get_barrier_semaphore()

    @pl.loop(1, n)
    def _(off):
        pl.semaphore_signal(
            barrier,
            inc=1,
            device_id={"dap": lax.rem(me + off, n)},
            device_id_type=pl.DeviceIdType.MESH,
        )

    def copy(phase, far, src, dst, to, source):
        base, slot = (far_base, parts) if far else (own_base, 0)
        return pltpu.make_async_remote_copy(
            src_ref=src,
            dst_ref=dst,
            send_sem=send_sem.at[phase, slot + to],
            recv_sem=recv_sem.at[phase, slot + source],
            device_id={"dap": base + to},
            device_id_type=pl.DeviceIdType.MESH,
        )

    def turn(t):
        return lax.rem(mine + t, parts)

    def at_rows(d):
        return pl.ds(pl.multiple_of(d * ROWS, ROWS), ROWS)

    def at_blocks(d, size):
        return pl.ds(pl.multiple_of(d * size, size), size)

    def grouped(values):
        return values.reshape(values.shape[0] // ROWS, ROWS, length)

    load.wait()
    mask_f = held[pl.ds(2 * size + 6 * chans, 2 * ROWS), :].astype(F32)
    gate_t = interleaved(w_a_gate, w_b_gate, parts)
    proj_t = interleaved(w_a_proj, w_b_proj, parts)
    gate_tb, proj_tb = gate_t.astype(BF16), proj_t.astype(BF16)
    for i in range(ROWS):
        x = pair[i][...].astype(F32).T
        mu = jnp.mean(x, axis=0, keepdims=True)
        inv = lax.rsqrt(jnp.mean(x * x, axis=0, keepdims=True) - mu * mu + 1e-05)
        normed = (x - mu) * inv
        normed_s[i] = normed
        inv_s[i] = inv
        nb_s[i] = normed.astype(BF16)

    few = parts // 2
    for g in range(2):
        rows = slice(g * chans, (g + 1) * chans)
        for i in range(ROWS):
            gate = jax.nn.sigmoid(matmul(gate_tb[rows], nb_s[i]))
            proj = matmul(proj_tb[rows], nb_s[i])
            gate_s[i, rows] = gate
            proj_s[i, rows] = proj
            masked = mask_f[i : i + 1, :]
            pos_buf[pl.ds(g * chans * ROWS + i, chans, stride=ROWS), :] = gate * proj * masked
        if g == 0:
            pl.semaphore_wait(barrier, n - 1)

        @pl.loop(0, few)
        def _(t):
            q = g * few + lax.rem(mine + t, few)
            send1[q] = pos_buf[at_blocks(q, 2 * block), :].astype(BF16)
            copy(0, True, send1.at[q, pl.ds(block, block)], far1.at[mine], q, mine).start()

            @pl.when(q != mine)
            def _():
                copy(0, False, send1.at[q], recv1.at[mine], q, mine).start()

    og_t = transposed(w_gate).astype(BF16)
    for i in range(ROWS):
        gate = jax.nn.sigmoid(matmul(og_t, nb_s[i]))
        d_upd = cotangent[i][...].astype(F32).T * gate
        dtrin_s[i] = matmul(w_out[...], d_upd.astype(BF16))
        og_s[i] = d_upd * (1.0 - gate)

    def keep(s, values):
        values = grouped(values.astype(F32))
        left_s[:, at_rows(s), :] = values[:width]
        right_s[:, at_rows(own_base + s), :] = values[width:]

    keep(mine, send1[mine])

    @pl.loop(1, parts)
    def _(t):
        s = turn(t)
        copy(0, False, send1.at[s], recv1.at[s], s, s).wait_recv()
        keep(s, recv1[s])

    @pl.loop(0, parts)
    def _(t):
        s = turn(t)
        copy(0, True, send1.at[s, pl.ds(block, block)], far1.at[s], s, s).wait_recv()
        right_s[:, at_rows(far_base + s), :] = grouped(far1[s].astype(F32))

    for c in range(width):
        tri_s[c] = lax.dot_general(
            left_s[c].astype(BF16),
            right_s[c].astype(BF16),
            (((1,), (1,)), ((), ())),
            preferred_element_type=F32,
        )

    def tri_block(q):
        return tri_s[:, at_rows(q), :].reshape(block, length)

    @pl.loop(1, parts)
    def _(t):
        q = turn(t)
        send2[q] = tri_block(q).astype(BF16)
        copy(1, False, send2.at[q], recv2.at[mine], q, mine).start()

    pos_buf[at_blocks(mine, block), :] = tri_block(mine)

    @pl.loop(1, parts)
    def _(t):
        s = turn(t)
        copy(1, False, send2.at[s], recv2.at[s], s, s).wait_recv()
        pos_buf[at_blocks(s, block), :] = recv2[s].astype(F32)

    out_t = transposed(w_out).astype(BF16)
    for i in range(ROWS):
        rows = pl.ds(i, chans, stride=ROWS)
        tri = pos_buf[rows, :]
        mean_h = jnp.mean(tri, axis=0, keepdims=True)
        inv_h = lax.rsqrt(jnp.mean(tri * tri, axis=0, keepdims=True) - mean_h * mean_h + 1e-05)
        tri_n = (tri - mean_h) * inv_h
        update = matmul(out_t, tri_n.astype(BF16))
        dpre_s[i] = (og_s[i] * update).astype(BF16)
        d_trin = dtrin_s[i]
        one = jnp.mean(d_trin, axis=0, keepdims=True)
        two = jnp.mean(d_trin * tri_n, axis=0, keepdims=True)
        pos_buf[rows, :] = inv_h * (d_trin - one - tri_n * two)

    @pl.loop(1, parts)
    def _(t):
        q = turn(t)
        send3[q] = pos_buf[at_blocks(q, block), :].astype(BF16)
        copy(2, False, send3.at[q], recv3.at[mine], q, mine).start()

    tri_s[:, at_rows(mine), :] = grouped(pos_buf[at_blocks(mine, block), :])

    @pl.loop(1, parts)
    def _(t):
        s = turn(t)
        copy(2, False, send3.at[s], recv3.at[s], s, s).wait_recv()
        tri_s[:, at_rows(s), :] = grouped(recv3[s].astype(F32))

    for c in range(width):
        dright_s[c] = matmul(tri_s[c].T.astype(BF16), left_s[c].astype(BF16))

    @pl.loop(0, parts)
    def _(t):
        q = turn(t)
        sfar4[q] = dright_s[:, at_rows(far_base + q), :].reshape(block, length).astype(BF16)
        copy(3, True, sfar4.at[q], far4.at[mine], q, mine).start()

    for c in range(width):
        dleft_s[c] = matmul(tri_s[c].astype(BF16), right_s[c].astype(BF16))

    def grad_blocks(q):
        return (
            dleft_s[:, at_rows(q), :].reshape(block, length),
            dright_s[:, at_rows(own_base + q), :].reshape(block, length),
        )

    @pl.loop(1, parts)
    def _(t):
        q = turn(t)
        d_left, d_right = grad_blocks(q)
        send4[q, pl.ds(0, block)] = d_left.astype(BF16)
        send4[q, pl.ds(block, block)] = d_right.astype(BF16)
        copy(3, False, send4.at[q], recv4.at[mine], q, mine).start()

    d_left, d_right = grad_blocks(mine)
    pos_buf[at_blocks(2 * mine, block), :] = d_left
    pos_buf[at_blocks(2 * mine + 1, block), :] = d_right
    gate_w, proj_w = gate_t.T.astype(BF16), proj_t.T.astype(BF16)

    @pl.loop(1, parts)
    def _(t):
        s = turn(t)
        copy(3, False, send4.at[s], recv4.at[s], s, s).wait_recv()
        pos_buf[at_blocks(s, 2 * block), :] = recv4[s].astype(F32)

    @pl.loop(0, parts)
    def _(t):
        s = turn(t)
        copy(3, True, sfar4.at[s], far4.at[s], s, s).wait_recv()
        pos_buf[at_blocks(2 * s + 1, block), :] += far4[s].astype(F32)

    for i in range(ROWS):
        grad = pos_buf[pl.ds(i, 2 * chans, stride=ROWS), :] * mask_f[i : i + 1, :]
        gate = gate_s[i]
        d_proj = grad * gate
        d_gate = d_proj * proj_s[i] * (1.0 - gate)
        d_normed = (
            matmul(gate_w, d_gate.astype(BF16))
            + matmul(proj_w, d_proj.astype(BF16))
            + matmul(w_gate[...], dpre_s[i])
        )
        normed = normed_s[i]
        out[i] = inv_s[i] * (
            d_normed
            - jnp.mean(d_normed, axis=0, keepdims=True)
            - normed * jnp.mean(d_normed * normed, axis=0, keepdims=True)
        )

    @pl.loop(0, parts)
    def _(q):
        copy(0, True, send1.at[q, pl.ds(block, block)], far1.at[q], q, q).wait_send()
        copy(3, True, sfar4.at[q], far4.at[q], q, q).wait_send()

    @pl.loop(1, parts)
    def _(t):
        q = turn(t)
        copy(0, False, send1.at[q], recv1.at[q], q, q).wait_send()
        copy(1, False, send2.at[q], recv2.at[q], q, q).wait_send()
        copy(2, False, send3.at[q], recv3.at[q], q, q).wait_send()
        copy(3, False, send4.at[q], recv4.at[q], q, q).wait_send()


def fused_shards(n, *args):
    rows, length, chans = args[0].shape
    parts = n // 2
    width = chans // parts
    block = width * rows

    pair, cotangent, pair_mask = args[:3]
    packed = jnp.concatenate(
        [pair.reshape(-1, chans), cotangent.reshape(-1, chans), *args[3:]]
        + [pair_mask.astype(BF16), jnp.zeros((ROWS, length), BF16)]
    )

    def vmem(dtype, *shape):
        return pltpu.VMEM(shape, dtype)

    grad_t = pl.pallas_call(
        functools.partial(fused_kernel, n),
        out_shape=jax.ShapeDtypeStruct((rows, chans, length), F32),
        in_specs=[pl.BlockSpec(memory_space=pltpu.HBM)],
        out_specs=pl.BlockSpec(memory_space=pltpu.VMEM),
        scratch_shapes=[
            vmem(BF16, *packed.shape),
            vmem(F32, rows, chans, length),
            vmem(BF16, rows, chans, length),
            vmem(F32, rows, 1, length),
            vmem(F32, rows, 2 * chans, length),
            vmem(F32, rows, 2 * chans, length),
            vmem(F32, rows, chans, length),
            vmem(F32, rows, chans, length),
            vmem(BF16, rows, chans, length),
            vmem(F32, 2 * chans * rows, length),
            vmem(F32, width, parts * rows, length),
            vmem(F32, width, length, length),
            vmem(F32, width, parts * rows, length),
            vmem(F32, width, parts * rows, length),
            vmem(F32, width, length, length),
            vmem(BF16, parts, 2 * block, length),
            vmem(BF16, parts, 2 * block, length),
            vmem(BF16, parts, block, length),
            vmem(BF16, parts, block, length),
            vmem(BF16, parts, block, length),
            vmem(BF16, parts, block, length),
            vmem(BF16, parts, block, length),
            vmem(BF16, parts, 2 * block, length),
            vmem(BF16, parts, 2 * block, length),
            vmem(BF16, parts, block, length),
            vmem(BF16, parts, block, length),
            pltpu.SemaphoreType.DMA((4, n)),
            pltpu.SemaphoreType.DMA((4, n)),
            pltpu.SemaphoreType.DMA,
        ],
        compiler_params=pltpu.CompilerParams(
            collective_id=0, has_side_effects=True, vmem_limit_bytes=48 * 1024 * 1024
        ),
    )(packed)
    return jnp.swapaxes(grad_t, 1, 2)


def body_for(mesh):
    n = mesh.shape["dap"]

    def body(*args):
        rows, length, chans = args[0].shape
        fits = mesh.shape["ch"] == 1 and n == 16 and rows == ROWS
        if fits and length == rows * n == chans:
            return fused_shards(n, *args)
        return shards(*args)

    return body


def solution(mesh):
    return jax.shard_map(
        body_for(mesh),
        mesh=mesh,
        in_specs=(
            P(("grp", "dap"), None, None),
            P(("grp", "dap"), None, None),
            P(("grp", "dap"), None),
            P(None, "ch"),
            P(None, "ch"),
            P(None, "ch"),
            P(None, "ch"),
            P(),
            P("ch", None),
        ),
        out_specs=P(("grp", "dap"), None, None),
        check_vma=False,
    )
```
